256 devices in a mesh: replica: 8 (over x_hi, y), shard: 32 (over x_lo, z, core).
Axes of the slice: x: 4 (x_hi: 2, x_lo: 2; x = x_hi * 2 + x_lo), y: 4, z: 8, core: 2. Of those that a mesh axis runs over, the one named last changes fastest.
Arguments:
- gradients: bfloat16 [8, 32, 512, 4608], P('replica', 'shard'), may hold values from -96 to 96
- master: float32 [512, 4608], P('shard'), may hold values from -0.12 to 0.12
- moment1: float32 [512, 4608], P('shard'), may hold values from -0.6 to 0.6
- moment2: float32 [512, 4608], P('shard'), may hold values from 0.1 to 2
Outputs:
- master_new: float32 [512, 4608], P('shard')
- moment1_new: float32 [512, 4608], P('shard')
- moment2_new: float32 [512, 4608], P('shard')
- params: bfloat16 [512, 4608], replicated
The draws below stay inside these ranges and needn't reach their ends.
All inputs are finite; a program needn't handle non-finite values.
Results may differ from the reference program's by a relative error of at most 0.0004.
Values may be sent and summed in bfloat16 or wider, within the bound.
No kernel may reach another device: no remote copies, remote signals or barrier semaphores. Data moves between devices by JAX's collectives and lax.ppermute only.
A program may use at most 128 MiB of HBM per device.

```python
import math
import jax
import jax.numpy as jnp
from jax import lax

D = 4608
STEP = 10
ROWS = 512
N_REPLICA = 8
N_SHARD = 32


def signed_band(key, lower, upper):
    sign_key, size_key = jax.random.split(key)
    signs = jnp.where(jax.random.bernoulli(sign_key, 0.5, (ROWS, D)), 1.0, -1.0).astype(jnp.float32)
    sizes = jax.random.uniform(size_key, (ROWS, D), jnp.float32, lower, upper)
    return signs * sizes


def draw_master(key, part):
    key = jax.random.fold_in(key, 11)
    return signed_band(key, 0.068, 0.118)


def strengthened(result, rng, source, target, parts, factor):
    owner, partner = [(jnp.arange(result.shape[axis_at]) // (result.shape[axis_at] // parts)).reshape([-1 if axis == axis_at else 1 for axis in range(result.ndim)]) for axis_at in (source, target)]
    chosen = jax.random.permutation(rng, parts)[partner]
    strong = (owner == chosen) | (owner == (partner + parts // 2) % parts)
    return jnp.where(strong, factor * result, result)


def shard_levels(key, shape, shards, low, largest):
    loudness, own = 1.0, jax.random.fold_in(key, 6)
    for position, shards_of in shards:
        draws = jnp.exp(jax.random.uniform(jax.random.fold_in(own, position), (shards_of,), jnp.float32, low / len(shards), largest / len(shards)))
        loudness = loudness * jnp.repeat(draws, shape[position] // shards_of).reshape([-1 if axis == position else 1 for axis in range(len(shape))])
    return loudness


def noise(own_key, extent, scale, bound, cuts=(), dtype=jnp.bfloat16):
    entries = scale * jax.random.normal(own_key, extent, jnp.float32)
    if cuts:
        entries = entries * shard_levels(own_key, extent, cuts, -0.22, 0.18)
    return jnp.clip(entries, -bound, bound).astype(dtype)


def heavy_noise(own_key, dims, spread, most, pieces, heavy, kind=jnp.bfloat16):
    array = spread * jax.random.normal(own_key, dims, jnp.float32)
    if pieces:
        array = array * shard_levels(own_key, dims, pieces, -0.22, 0.18)
    return jnp.clip(strengthened(array, jax.random.fold_in(own_key, 3), *heavy), -most, most).astype(kind)


def setup_inputs(seed: int = 0) -> dict:
    streams_of = jax.random.split(jax.random.key(seed), 5)
    return {
        "gradients": heavy_noise(streams_of[0], (N_REPLICA, N_SHARD, ROWS, D), ((N_REPLICA * N_SHARD) ** 0.5), 96.0, ((0, 8), (1, 32)), (1, 2, 32, 2.75)),
        "master": draw_master(jax.random.fold_in(streams_of[4], 71), 0),
        "moment1": noise(streams_of[2], (ROWS, D), 0.1, 0.6, ((0, 32),), jnp.float32),
        "moment2": jnp.clip(jnp.exp(math.log(2.0) - 2.9957323 * jax.random.uniform(streams_of[3], (ROWS, D), jnp.float32) ** shard_levels(streams_of[3], (ROWS, D), ((0, 32),), -0.2, 0.2)), 0.1, 2.0),
    }


def reference(gradients, master, moment1, moment2):
    flat = gradients.reshape(N_REPLICA * N_SHARD, ROWS, D)

    def add_one(total, piece):
        return (total + piece.astype(jnp.float32), None)
    total, unused = lax.scan(add_one, jnp.zeros((ROWS, D), jnp.float32), flat)
    grad = total / (N_REPLICA * N_SHARD)
    moment1_new = 0.9 * moment1 + 0.1 * grad
    moment2_new = 0.95 * moment2 + 0.05 * grad * grad
    first_fix = 1.0 - 0.9 ** STEP
    second_fix = 1.0 - 0.95 ** STEP
    update = moment1_new / first_fix / (jnp.sqrt(moment2_new / second_fix) + 1e-08)
    master_new = master * (1.0 - 0.02 * 0.1) - 0.02 * update
    params = master_new.astype(jnp.bfloat16)
    return (master_new, moment1_new, moment2_new, params)
```

```python
import jax
import jax.numpy as jnp
from jax import lax
from jax.sharding import Mesh, PartitionSpec as P

STEP = 10
PLANE = ("xh", "y", "xl")
SWAP = [(0, 1), (1, 0)]


def adam(grad, master, moment1, moment2):
    moment1_new = 0.9 * moment1 + 0.1 * grad
    moment2_new = 0.95 * moment2 + 0.05 * grad * grad
    first_fix = 1.0 - 0.9**STEP
    second_fix = 1.0 - 0.95**STEP
    update = moment1_new / first_fix / (jnp.sqrt(moment2_new / second_fix) + 1e-08)
    master_new = master * (1.0 - 0.02 * 0.1) - 0.02 * update
    return master_new, moment1_new, moment2_new


def gather(piece, axes, n):
    return lax.all_to_all(jnp.broadcast_to(piece, (n, *piece.shape)), axes, 0, 0, tiled=True)


def per_device(gradients, master, moment1, moment2):
    xh, y, core = (lax.axis_index(a) for a in ("xh", "y", "c"))
    n_xh, n_y, n_xl, n_z = (lax.axis_size(a) for a in ("xh", "y", "xl", "z"))
    rows, width = gradients.shape[2:]
    own = master.shape[0]
    low, cols = own // n_xh, width // n_y
    blocks = n_xl * n_z
    plane = n_xh * n_y * n_xl
    local = gradients.reshape(blocks, 2, own, width)

    mine = lax.dynamic_index_in_dim(local, core, 1, keepdims=False)
    theirs = lax.dynamic_index_in_dim(local, 1 - core, 1, keepdims=False)
    came = lax.ppermute(theirs, "c", SWAP)
    pair = (mine.astype(jnp.float32) + came.astype(jnp.float32)).astype(jnp.float16)
    pair = pair.reshape(n_xl, n_z, n_xh, low, n_y, cols).transpose(2, 4, 0, 1, 3, 5)
    pair = pair.reshape(plane, n_z, low, cols)

    pair = lax.all_to_all(pair, PLANE, 0, 0, tiled=True)
    column = jnp.sum(pair.astype(jnp.float32), axis=0).astype(jnp.float16)
    column = lax.all_to_all(column, "z", 0, 0, tiled=True)
    grad = jnp.sum(column.astype(jnp.float32), axis=0) / (plane * n_z * 2)

    def piece(state):
        state = state.reshape(n_xh, low, n_y, cols)
        return lax.dynamic_index_in_dim(
            lax.dynamic_index_in_dim(state, xh, 0, keepdims=False), y, 1, keepdims=False
        )

    part = adam(grad, piece(master), piece(moment1), piece(moment2))[0].astype(jnp.bfloat16)
    part = gather(part, "z", n_z)
    part = gather(part, PLANE, plane)
    part = part.reshape(n_xh, n_y, n_xl, n_z, low, cols).transpose(2, 3, 0, 4, 1, 5)
    part = part.reshape(blocks, own, width)
    other = lax.ppermute(part, "c", SWAP)
    first = core == 0
    params = jnp.stack([jnp.where(first, part, other), jnp.where(first, other, part)], axis=1)

    whole = gather(grad, ("xh", "y"), n_xh * n_y)
    whole = whole.reshape(n_xh, n_y, low, cols).transpose(0, 2, 1, 3).reshape(own, width)
    master_new, moment1_new, moment2_new = adam(whole, master, moment1, moment2)
    return master_new, moment1_new, moment2_new, params.reshape(rows, width)


def solution(mesh):
    fine = Mesh(mesh.devices.reshape(2, 4, 2, 8, 2), ("xh", "y", "xl", "z", "c"))
    replica, shard = ("xh", "y"), ("xl", "z", "c")
    state = P(shard, None)
    return jax.shard_map(
        per_device,
        mesh=fine,
        in_specs=(P(replica, shard, None, None), state, state, state),
        out_specs=(state, state, state, P()),
        check_vma=False,
    )
```

```python
import jax
import jax.numpy as jnp
from jax import lax
from jax.experimental import pallas as pl
from jax.experimental.pallas import tpu as pltpu
from jax.sharding import Mesh, PartitionSpec as P

STEP = 10
XH, Y, XL, Z, CORES = 2, 4, 2, 8, 2
PLANE = ("xh", "y", "xl")
SWAP = [(0, 1), (1, 0)]
OWN = 16
PIECE = 384
LEFT, RIGHT = XH * Y, Y
BLOCKS = XL * Z
VMEM = pl.BlockSpec(memory_space=pltpu.VMEM)
ANY = pl.BlockSpec(memory_space=pl.ANY)


def columns(i):
    return pl.ds(i * PIECE, PIECE)


def views(whole, left, right, core):
    pairs = [(whole.at[:, core, :, columns(i)], left.at[i]) for i in range(LEFT)]
    for y in range(RIGHT):
        for xl in range(XL):
            block = whole.at[pl.ds(xl * Z, Z), core, :, columns(LEFT + y)]
            pairs.append((block, right.at[:, y, xl]))
    return pairs


N_VIEWS = LEFT + RIGHT * XL
LEFT_SHAPE = (LEFT, BLOCKS, OWN, PIECE)
RIGHT_SHAPE = (Z, RIGHT, XL, OWN, PIECE)


def run(copies):
    for copy in copies:
        copy.start()
    for copy in copies:
        copy.wait()


def split_mine_kernel(whole, left, right, sems):
    pairs = views(whole, left, right, lax.axis_index("c"))
    run([pltpu.make_async_copy(a, b, sems.at[k]) for k, (a, b) in enumerate(pairs)])


def split_theirs_kernel(whole, left, right, sems):
    pairs = views(whole, left, right, 1 - lax.axis_index("c"))
    run([pltpu.make_async_copy(a, b, sems.at[k]) for k, (a, b) in enumerate(pairs)])


def split(kernel, name, grad):
    return pl.pallas_call(
        kernel,
        out_shape=[pltpu.VMEM(s, grad.dtype) for s in (LEFT_SHAPE, RIGHT_SHAPE)],
        in_specs=[ANY],
        out_specs=[ANY] * 2,
        scratch_shapes=[pltpu.SemaphoreType.DMA((N_VIEWS,))],
        cost_estimate=pl.CostEstimate(flops=0, bytes_accessed=2 * grad.size, transcendentals=0),
        name=name,
    )(grad)


def place_mine_kernel(left, right, out, sems):
    pairs = views(out, left, right, lax.axis_index("c"))
    run([pltpu.make_async_copy(b, a, sems.at[k]) for k, (a, b) in enumerate(pairs)])


def place_theirs_kernel(half, left, right, out, sems):
    pairs = views(out, left, right, 1 - lax.axis_index("c"))
    run([pltpu.make_async_copy(b, a, sems.at[k]) for k, (a, b) in enumerate(pairs)])


def in_vmem(a):
    return pltpu.with_memory_space_constraint(a, pltpu.VMEM)


def place(kernel, name, left, right, half=()):
    shape = jax.ShapeDtypeStruct((BLOCKS, CORES, OWN, (LEFT + RIGHT) * PIECE), left.dtype)
    return pl.pallas_call(
        kernel,
        out_shape=shape,
        in_specs=[ANY] * (len(half) + 2),
        out_specs=ANY,
        scratch_shapes=[pltpu.SemaphoreType.DMA((N_VIEWS,))],
        input_output_aliases={0: 0} if half else {},
        cost_estimate=pl.CostEstimate(flops=0, bytes_accessed=6 * left.size, transcendentals=0),
        name=name,
    )(*half, in_vmem(left), in_vmem(right))


def join_kernel(*refs):
    out, sems, z = refs[Z], refs[Z + 1], lax.axis_index("z")
    run([pltpu.make_async_copy(refs[d], out.at[lax.rem(z - d + Z, Z)], sems.at[d]) for d in range(Z)])


def join(arrays):
    size = Z * arrays[0].size
    return pl.pallas_call(
        join_kernel,
        out_shape=pltpu.VMEM((Z, *arrays[0].shape), arrays[0].dtype),
        in_specs=[ANY] * Z,
        out_specs=ANY,
        scratch_shapes=[pltpu.SemaphoreType.DMA((Z,))],
        cost_estimate=pl.CostEstimate(flops=0, bytes_accessed=4 * size, transcendentals=0),
        name="join",
    )(*[in_vmem(a) for a in arrays])


def spread_kernel(*refs):
    out, z = refs[Z], lax.axis_index("z")
    for d in range(Z):
        piece = refs[d][...]
        for p in range(out.shape[0]):
            out[p, lax.rem(z - d + Z, Z)] = piece


def spread(pieces):
    shape = (XH * Y * XL, Z, OWN, PIECE)
    return pl.pallas_call(
        spread_kernel,
        out_shape=pltpu.VMEM(shape, pieces[0].dtype),
        in_specs=[VMEM] * Z,
        out_specs=VMEM,
        cost_estimate=pl.CostEstimate(flops=0, bytes_accessed=2 * XH * Y * XL * Z * OWN * PIECE, transcendentals=0),
        name="spread",
    )(*[in_vmem(a) for a in pieces])


def adam(grad, master, moment1, moment2):
    moment1_new = 0.9 * moment1 + 0.1 * grad
    moment2_new = 0.95 * moment2 + 0.05 * grad * grad
    first_fix = 1.0 - 0.9**STEP
    second_fix = 1.0 - 0.95**STEP
    update = moment1_new / first_fix / (jnp.sqrt(moment2_new / second_fix) + 1e-08)
    master_new = master * (1.0 - 0.02 * 0.1) - 0.02 * update
    return master_new, moment1_new, moment2_new


def states_kernel(own, other, master, moment1, moment2, master_new, moment1_new, moment2_new):
    xh, y = lax.axis_index("xh"), lax.axis_index("y")
    for k in range(Y):
        at_y = y ^ k
        grads = [(own[2 * k], Y * xh + at_y), (own[2 * k + 1], LEFT + at_y), (other[k], Y * (1 - xh) + at_y)]
        for grad, i in grads:
            at = (slice(None), pl.ds(pl.multiple_of(i * PIECE, 128), PIECE))
            new = adam(grad, master[at], moment1[at], moment2[at])
            master_new[at], moment1_new[at], moment2_new[at] = new


def states(own, other, master, moment1, moment2):
    return pl.pallas_call(
        states_kernel,
        out_shape=[jax.ShapeDtypeStruct(master.shape, master.dtype)] * 3,
        in_specs=[VMEM] * 5,
        out_specs=[VMEM] * 3,
        cost_estimate=pl.CostEstimate(flops=20 * master.size, bytes_accessed=28 * master.size, transcendentals=master.size),
        name="states",
    )(own, other, master, moment1, moment2)


def exchange(chunks, axes):
    return lax.all_to_all(chunks, axes, 0, 0, tiled=True)


def gather(piece, axes, n):
    return exchange(jnp.broadcast_to(piece, (n, *piece.shape)), axes)


def forward(chunk, d):
    return lax.ppermute(chunk, "z", [(z, (z + d) % Z) for z in range(Z)])


def along_z(piece):
    return [piece] + [forward(piece, d) for d in range(1, Z)]


def add(parts):
    return jnp.sum(parts.astype(jnp.float32), axis=0)


def half_width(a):
    return a.astype(jnp.float16)


def per_device(gradients, master, moment1, moment2):
    xh, y, z = (lax.axis_index(a) for a in ("xh", "y", "z"))
    rows, width = gradients.shape[2:]
    plane = XH * Y * XL
    local = gradients.reshape(BLOCKS, CORES, OWN, width)

    def ahead(chunks, d):
        return lax.dynamic_index_in_dim(chunks, lax.rem(z + d, Z), 0, keepdims=False)

    def sum_along_z(chunk_of):
        total = chunk_of(0).astype(jnp.float32)
        for d in range(1, Z):
            total = total + forward(chunk_of(d), d).astype(jnp.float32)
        return total

    their_left, their_right = split(split_theirs_kernel, "split_theirs", local)
    came_right = lax.ppermute(their_right, "c", SWAP)
    came_left = lax.ppermute(their_left, "c", SWAP)
    my_left, my_right = split(split_mine_kernel, "split_mine", local)

    def right_chunk(d):
        return half_width(ahead(my_right, d).astype(jnp.float32) + ahead(came_right, d).astype(jnp.float32))

    right = half_width(sum_along_z(right_chunk))
    left = half_width(my_left.astype(jnp.float32) + came_left.astype(jnp.float32))
    left = half_width(add(exchange(left.reshape(plane, Z, OWN, PIECE), PLANE)))
    left = sum_along_z(lambda d: ahead(left, d))
    right = jnp.broadcast_to(right, (XH, *right.shape)).reshape(plane, OWN, PIECE)
    right = add(exchange(right, PLANE))
    count = plane * Z * CORES
    left, right = left / count, right / count

    def new(grad, i):
        at = [lax.dynamic_slice_in_dim(a, i * PIECE, PIECE, 1) for a in (master, moment1, moment2)]
        return adam(grad, *at)[0].astype(jnp.bfloat16)

    lefts = along_z(new(left, Y * xh + y))
    new_right = gather(new(right, LEFT + y), ("y", "xl"), Y * XL).reshape(Y, XL, OWN, PIECE)
    lefts, new_right = lax.optimization_barrier((lefts, new_right))
    rights = along_z(new_right)
    new_left = exchange(spread(lefts), PLANE).reshape(LEFT_SHAPE)
    new_right = join(rights)

    own = jnp.stack([left, right])
    own = jnp.concatenate([own, lax.ppermute(own, "y", [(i, i ^ 1) for i in range(Y)])])
    own = jnp.concatenate([own, lax.ppermute(own, "y", [(i, i ^ 2) for i in range(Y)])])
    other = lax.ppermute(own.reshape(Y, 2, OWN, PIECE)[:, 0], "xh", SWAP)

    new_left, new_right, other = lax.optimization_barrier((new_left, new_right, other))
    their_right = lax.ppermute(new_right, "c", SWAP)
    their_left = lax.ppermute(new_left, "c", SWAP)
    half = place(place_mine_kernel, "place_mine", new_left, new_right)
    params = place(place_theirs_kernel, "place_theirs", their_left, their_right, (half,))
    master_new, moment1_new, moment2_new = states(own, other, master, moment1, moment2)
    return master_new, moment1_new, moment2_new, params.reshape(rows, width)


def solution(mesh):
    fine = Mesh(mesh.devices.reshape(XH, Y, XL, Z, CORES), ("xh", "y", "xl", "z", "c"))
    replica, shard = ("xh", "y"), ("xl", "z", "c")
    state = P(shard, None)
    return jax.shard_map(
        per_device,
        mesh=fine,
        in_specs=(P(replica, shard, None, None), state, state, state),
        out_specs=(state, state, state, P()),
        check_vma=False,
    )
```

```python
import jax
import jax.numpy as jnp
from jax import lax
from jax.experimental import pallas as pl
from jax.experimental.pallas import tpu as pltpu
from jax.sharding import Mesh, PartitionSpec as P

STEP = 10
XH, Y, XL, Z, CORES = 2, 4, 2, 8, 2
PLANE = ("xh", "y", "xl")
SWAP = [(0, 1), (1, 0)]
LOW, COLS = 8, 1152
PIECES, BLOCKS = XH * Y, XL * Z
SHAPE = (PIECES, BLOCKS, LOW, COLS)
WHOLE = (BLOCKS, CORES, XH, LOW, Y * COLS)
VMEM = pl.BlockSpec(memory_space=pltpu.VMEM)
ANY = pl.BlockSpec(memory_space=pl.ANY)
SMALL = pltpu.CompilerParams(vmem_limit_bytes=2 * 2**20)


def views(whole, core):
    return [
        whole.at[:, core, xh, :, pl.ds(y * COLS, COLS)] for xh in range(XH) for y in range(Y)
    ]


def copy_all(sources, targets, sems):
    copies = [
        pltpu.make_async_copy(a, b, sems.at[k]) for k, (a, b) in enumerate(zip(sources, targets))
    ]
    for copy in copies:
        copy.start()
    for copy in copies:
        copy.wait()


def split_kernel(of_other, whole, pieces, sems):
    core = lax.axis_index("c")
    sources = views(whole, 1 - core if of_other else core)
    copy_all(sources, [pieces.at[i] for i in range(PIECES)], sems)


def split(of_other, whole):
    return pl.pallas_call(
        lambda *refs: split_kernel(of_other, *refs),
        out_shape=pltpu.VMEM(SHAPE, whole.dtype),
        in_specs=[ANY],
        out_specs=ANY,
        scratch_shapes=[pltpu.SemaphoreType.DMA((PIECES,))],
        compiler_params=SMALL,
        cost_estimate=pl.CostEstimate(flops=0, bytes_accessed=2 * whole.size, transcendentals=0),
        name="split_theirs" if of_other else "split_mine",
    )(whole)


def place_kernel(of_other, *refs):
    pieces, out, sems = refs[-3:]
    core = lax.axis_index("c")
    targets = views(out, 1 - core if of_other else core)
    copy_all([pieces.at[i] for i in range(PIECES)], targets, sems)


def place(of_other, pieces, half=()):
    return pl.pallas_call(
        lambda *refs: place_kernel(of_other, *refs),
        out_shape=jax.ShapeDtypeStruct(WHOLE, pieces.dtype),
        in_specs=[ANY] * (len(half) + 1),
        out_specs=ANY,
        scratch_shapes=[pltpu.SemaphoreType.DMA((PIECES,))],
        input_output_aliases={0: 0} if half else {},
        compiler_params=SMALL,
        cost_estimate=pl.CostEstimate(flops=0, bytes_accessed=4 * pieces.size, transcendentals=0),
        name="place_theirs" if of_other else "place_mine",
    )(*half, pltpu.with_memory_space_constraint(pieces, pltpu.VMEM))


def adam(grad, master, moment1, moment2):
    moment1_new = 0.9 * moment1 + 0.1 * grad
    moment2_new = 0.95 * moment2 + 0.05 * grad * grad
    first_fix = 1.0 - 0.9**STEP
    second_fix = 1.0 - 0.95**STEP
    update = moment1_new / first_fix / (jnp.sqrt(moment2_new / second_fix) + 1e-08)
    master_new = master * (1.0 - 0.02 * 0.1) - 0.02 * update
    return master_new, moment1_new, moment2_new


def states_kernel(mine, others, master, moment1, moment2, master_new, moment1_new, moment2_new):
    xh, y = lax.axis_index("xh"), lax.axis_index("y")
    for k in range(Y):
        for grad, low in ((mine[k], xh), (others[k], 1 - xh)):
            rows = pl.ds(pl.multiple_of(low * LOW, LOW), LOW)
            at = (rows, pl.ds(pl.multiple_of((y ^ k) * COLS, 128), COLS))
            new = adam(grad, master[at], moment1[at], moment2[at])
            master_new[at], moment1_new[at], moment2_new[at] = new


def states(mine, others, master, moment1, moment2):
    return pl.pallas_call(
        states_kernel,
        out_shape=[jax.ShapeDtypeStruct(master.shape, master.dtype)] * 3,
        in_specs=[VMEM] * 5,
        out_specs=[VMEM] * 3,
        compiler_params=pltpu.CompilerParams(vmem_limit_bytes=8 * 2**20),
        cost_estimate=pl.CostEstimate(
            flops=20 * master.size, bytes_accessed=28 * master.size, transcendentals=master.size
        ),
        name="states",
    )(mine, others, master, moment1, moment2)


def exchange(chunks, axes):
    return lax.all_to_all(chunks, axes, 0, 0, tiled=True)


def gather(piece, axes, n):
    return exchange(jnp.broadcast_to(piece, (n, *piece.shape)), axes)


def add(parts):
    return jnp.sum(parts.astype(jnp.float32), axis=0)


def per_device(gradients, master, moment1, moment2):
    xh, y = lax.axis_index("xh"), lax.axis_index("y")
    rows, width = gradients.shape[2:]
    plane = XH * Y * XL
    whole = pltpu.with_memory_space_constraint(gradients.reshape(WHOLE), pltpu.HBM)

    came = lax.ppermute(split(True, whole), "c", SWAP)
    pair = split(False, whole).astype(jnp.float32) + came.astype(jnp.float32)
    pair = pair.astype(jnp.float16).reshape(plane, Z, LOW, COLS)
    column = add(exchange(pair, PLANE)).astype(jnp.float16)
    grad = add(exchange(column, "z")) / (plane * Z * CORES)

    def piece(state):
        return lax.dynamic_slice(state, (xh * LOW, y * COLS), (LOW, COLS))

    part = adam(grad, piece(master), piece(moment1), piece(moment2))[0].astype(jnp.bfloat16)
    mine = jnp.stack([grad])
    came = lax.ppermute(mine, "y", [(i, i ^ 1) for i in range(Y)])
    part, came = lax.optimization_barrier((gather(part, "z", Z), came))
    mine = jnp.concatenate([mine, came])
    came = lax.ppermute(mine, "y", [(i, i ^ 2) for i in range(Y)])
    part, came = lax.optimization_barrier((gather(part, PLANE, plane), came))
    mine = jnp.concatenate([mine, came])
    others = lax.ppermute(mine, "xh", SWAP)
    part = part.reshape(SHAPE)
    came = lax.ppermute(part, "c", SWAP)
    params = place(True, came, (place(False, part),))
    master_new, moment1_new, moment2_new = states(mine, others, master, moment1, moment2)
    return master_new, moment1_new, moment2_new, params.reshape(rows, width)


def solution(mesh):
    fine = Mesh(mesh.devices.reshape(XH, Y, XL, Z, CORES), ("xh", "y", "xl", "z", "c"))
    replica, shard = ("xh", "y"), ("xl", "z", "c")
    state = P(shard, None)
    return jax.shard_map(
        per_device,
        mesh=fine,
        in_specs=(P(replica, shard, None, None), state, state, state),
        out_specs=(state, state, state, P()),
        check_vma=False,
    )
```

```python
import jax
import jax.numpy as jnp
from jax import lax
from jax.experimental import pallas as pl
from jax.experimental.pallas import tpu as pltpu
from jax.sharding import Mesh, PartitionSpec as P

STEP = 10
XH, Y, XL, ZH, ZL, CORES = 2, 4, 2, 4, 2, 2
BIG = ("xh", "y", "xl", "zl")
SWAP = [(0, 1), (1, 0)]
LOW, COLS = 8, 1152
SHAPE = (XH, Y, XL, ZL, ZH, LOW, COLS)
WHOLE = (XL, ZH, ZL, CORES, XH, LOW, Y * COLS)
COPIES = XH * Y * ZL
VMEM = pl.BlockSpec(memory_space=pltpu.VMEM)
ANY = pl.BlockSpec(memory_space=pl.ANY)
SMALL = pltpu.CompilerParams(vmem_limit_bytes=2 * 2**20)


def views(whole, pieces, core):
    return [
        (whole.at[:, :, zl, core, xh, :, pl.ds(y * COLS, COLS)], pieces.at[xh, y, :, zl])
        for xh in range(XH)
        for y in range(Y)
        for zl in range(ZL)
    ]


def copy_all(pairs, sems):
    copies = [pltpu.make_async_copy(a, b, sems.at[k]) for k, (a, b) in enumerate(pairs)]
    for copy in copies:
        copy.start()
    for copy in copies:
        copy.wait()


def split_kernel(of_other, whole, pieces, sems):
    core = lax.axis_index("c")
    copy_all(views(whole, pieces, 1 - core if of_other else core), sems)


def split(of_other, whole):
    return pl.pallas_call(
        lambda *refs: split_kernel(of_other, *refs),
        out_shape=pltpu.VMEM(SHAPE, whole.dtype),
        in_specs=[ANY],
        out_specs=ANY,
        scratch_shapes=[pltpu.SemaphoreType.DMA((COPIES,))],
        compiler_params=SMALL,
        cost_estimate=pl.CostEstimate(flops=0, bytes_accessed=2 * whole.size, transcendentals=0),
        name="split_theirs" if of_other else "split_mine",
    )(whole)


def place_kernel(of_other, *refs):
    pieces, out, sems = refs[-3:]
    core = lax.axis_index("c")
    pairs = views(out, pieces, 1 - core if of_other else core)
    copy_all([(b, a) for a, b in pairs], sems)


def place(of_other, pieces, half=()):
    return pl.pallas_call(
        lambda *refs: place_kernel(of_other, *refs),
        out_shape=jax.ShapeDtypeStruct(WHOLE, pieces.dtype),
        in_specs=[ANY] * (len(half) + 1),
        out_specs=ANY,
        scratch_shapes=[pltpu.SemaphoreType.DMA((COPIES,))],
        input_output_aliases={0: 0} if half else {},
        compiler_params=SMALL,
        cost_estimate=pl.CostEstimate(flops=0, bytes_accessed=4 * pieces.size, transcendentals=0),
        name="place_theirs" if of_other else "place_mine",
    )(*half, pltpu.with_memory_space_constraint(pieces, pltpu.VMEM))


def adam(grad, master, moment1, moment2):
    moment1_new = 0.9 * moment1 + 0.1 * grad
    moment2_new = 0.95 * moment2 + 0.05 * grad * grad
    first_fix = 1.0 - 0.9**STEP
    second_fix = 1.0 - 0.95**STEP
    update = moment1_new / first_fix / (jnp.sqrt(moment2_new / second_fix) + 1e-08)
    master_new = master * (1.0 - 0.02 * 0.1) - 0.02 * update
    return master_new, moment1_new, moment2_new


def states_kernel(*refs):
    pieces, old, new = refs[: XH * Y], refs[XH * Y : -3], refs[-3:]
    xh, y = lax.axis_index("xh"), lax.axis_index("y")
    for m, piece in enumerate(pieces):
        rows = pl.ds(pl.multiple_of((xh ^ (m // Y)) * LOW, LOW), LOW)
        at = (rows, pl.ds(pl.multiple_of((y ^ (m % Y)) * COLS, 128), COLS))
        for ref, value in zip(new, adam(piece[...], *[ref[at] for ref in old])):
            ref[at] = value


def states(pieces, master, moment1, moment2):
    return pl.pallas_call(
        states_kernel,
        out_shape=[jax.ShapeDtypeStruct(master.shape, master.dtype)] * 3,
        in_specs=[VMEM] * (XH * Y + 3),
        out_specs=[VMEM] * 3,
        compiler_params=pltpu.CompilerParams(vmem_limit_bytes=8 * 2**20),
        cost_estimate=pl.CostEstimate(
            flops=20 * master.size, bytes_accessed=28 * master.size, transcendentals=master.size
        ),
        name="states",
    )(*pieces, master, moment1, moment2)


def exchange(chunks):
    return lax.all_to_all(chunks.reshape(-1, ZH, LOW, COLS), BIG, 0, 0, tiled=True)


def forward(chunk, d):
    return lax.ppermute(chunk, "zh", [(i, (i + d) % ZH) for i in range(ZH)])


def add(parts):
    return jnp.sum(parts.astype(jnp.float32), axis=0)


def per_device(gradients, master, moment1, moment2):
    xh, y, zh = (lax.axis_index(a) for a in ("xh", "y", "zh"))
    rows, width = gradients.shape[2:]
    big = XH * Y * XL * ZL
    whole = pltpu.with_memory_space_constraint(gradients.reshape(WHOLE), pltpu.HBM)

    came = lax.ppermute(split(True, whole), "c", SWAP)
    pair = split(False, whole).astype(jnp.float32) + came.astype(jnp.float32)
    column = add(exchange(pair.astype(jnp.float16))).astype(jnp.float16)

    def ahead(d):
        return lax.dynamic_index_in_dim(column, lax.rem(zh + d, ZH), 0, keepdims=False)

    parts = [ahead(0)] + [forward(ahead(d), d) for d in range(1, ZH)]
    grad = sum(part.astype(jnp.float32) for part in parts) / (big * ZH * CORES)

    def piece(state):
        return lax.dynamic_slice(state, (xh * LOW, y * COLS), (LOW, COLS))

    part = adam(grad, piece(master), piece(moment1), piece(moment2))[0].astype(jnp.bfloat16)
    behind = [part] + [forward(part, d) for d in range(1, ZH)]
    behind = jnp.stack(behind[::-1] + behind[:0:-1])
    column = lax.dynamic_slice_in_dim(behind, ZH - 1 - zh, ZH, 0)
    part = exchange(jnp.broadcast_to(column, (big, *column.shape))).reshape(SHAPE)

    def across(m):
        return lax.ppermute(grad, ("xh", "y"), [(i, i ^ m) for i in range(XH * Y)])

    pieces = [grad] + [across(m) for m in range(1, XH * Y)]
    part, pieces = lax.optimization_barrier((part, pieces))

    came = lax.ppermute(part, "c", SWAP)
    params = place(True, came, (place(False, part),))
    master_new, moment1_new, moment2_new = states(pieces, master, moment1, moment2)
    return master_new, moment1_new, moment2_new, params.reshape(rows, width)


def solution(mesh):
    sizes = (XH, Y, XL, ZH, ZL, CORES)
    fine = Mesh(mesh.devices.reshape(sizes), ("xh", "y", "xl", "zh", "zl", "c"))
    replica, shard = ("xh", "y"), ("xl", "zh", "zl", "c")
    state = P(shard, None)
    return jax.shard_map(
        per_device,
        mesh=fine,
        in_specs=(P(replica, shard, None, None), state, state, state),
        out_specs=(state, state, state, P()),
        check_vma=False,
    )
```

```python
import jax
import jax.numpy as jnp
from jax import lax
from jax.experimental import pallas as pl
from jax.experimental.pallas import tpu as pltpu
from jax.sharding import Mesh, PartitionSpec as P

STEP = 10
XH, Y, XL, ZH, ZM, ZL, CORES = 2, 4, 2, 2, 2, 2, 2
BIG = ("xh", "y", "xl", "zl")
SWAP = [(0, 1), (1, 0)]
LOW, COLS = 8, 1152
SHAPE = (XH, Y, XL, ZL, ZH, ZM, LOW, COLS)
WHOLE = (XL, ZH, ZM, ZL, CORES, XH, LOW, Y * COLS)
COPIES = XH * Y * ZH * ZM
STATES = 3
VMEM = pl.BlockSpec(memory_space=pltpu.VMEM)
ANY = pl.BlockSpec(memory_space=pl.ANY)
SMALL = pltpu.CompilerParams(vmem_limit_bytes=2 * 2**20)


def views(whole, pieces, core):
    zh, zm = lax.axis_index("zh"), lax.axis_index("zm")
    return [
        (whole.at[:, zh ^ j, zm ^ k, :, core, xh, :, pl.ds(y * COLS, COLS)], pieces.at[xh, y, :, :, j, k])
        for xh in range(XH)
        for y in range(Y)
        for j in range(ZH)
        for k in range(ZM)
    ]


def copy_all(pairs, sems):
    copies = [pltpu.make_async_copy(a, b, sems.at[k]) for k, (a, b) in enumerate(pairs)]
    for copy in copies:
        copy.start()
    for copy in copies:
        copy.wait()


def split_theirs_kernel(whole, pieces, sems):
    copy_all(views(whole, pieces, 1 - lax.axis_index("c")), sems)


def split_mine_kernel(whole, master, moment1, moment2, pieces, olds, sems):
    rows = pl.ds(pl.multiple_of(lax.axis_index("xh") * LOW, LOW), LOW)
    cols = pl.ds(pl.multiple_of(lax.axis_index("y") * COLS, 128), COLS)
    states = [(state.at[rows, cols], olds.at[i]) for i, state in enumerate((master, moment1, moment2))]
    copy_all(views(whole, pieces, lax.axis_index("c")) + states, sems)


def split_theirs(whole):
    return pl.pallas_call(
        split_theirs_kernel,
        out_shape=pltpu.VMEM(SHAPE, whole.dtype),
        in_specs=[ANY],
        out_specs=ANY,
        scratch_shapes=[pltpu.SemaphoreType.DMA((COPIES,))],
        compiler_params=SMALL,
        cost_estimate=pl.CostEstimate(flops=0, bytes_accessed=2 * whole.size, transcendentals=0),
        name="split_theirs",
    )(whole)


def split_mine(whole, *states):
    return pl.pallas_call(
        split_mine_kernel,
        out_shape=[pltpu.VMEM(SHAPE, whole.dtype), pltpu.VMEM((STATES, LOW, COLS), jnp.float32)],
        in_specs=[ANY] * (1 + STATES),
        out_specs=[ANY] * 2,
        scratch_shapes=[pltpu.SemaphoreType.DMA((COPIES + STATES,))],
        compiler_params=SMALL,
        cost_estimate=pl.CostEstimate(flops=0, bytes_accessed=2 * whole.size, transcendentals=0),
        name="split_mine",
    )(whole, *states)


def place_kernel(of_other, *refs):
    pieces, out, sems = refs[-3:]
    core = lax.axis_index("c")
    pairs = views(out, pieces, 1 - core if of_other else core)
    copy_all([(b, a) for a, b in pairs], sems)


def place(of_other, pieces, half=()):
    return pl.pallas_call(
        lambda *refs: place_kernel(of_other, *refs),
        out_shape=jax.ShapeDtypeStruct(WHOLE, pieces.dtype),
        in_specs=[ANY] * (len(half) + 1),
        out_specs=ANY,
        scratch_shapes=[pltpu.SemaphoreType.DMA((COPIES,))],
        input_output_aliases={0: 0} if half else {},
        compiler_params=SMALL,
        cost_estimate=pl.CostEstimate(flops=0, bytes_accessed=4 * pieces.size, transcendentals=0),
        name="place_theirs" if of_other else "place_mine",
    )(*half, pltpu.with_memory_space_constraint(pieces, pltpu.VMEM))


def adam(grad, master, moment1, moment2):
    moment1_new = 0.9 * moment1 + 0.1 * grad
    moment2_new = 0.95 * moment2 + 0.05 * grad * grad
    first_fix = 1.0 - 0.9**STEP
    second_fix = 1.0 - 0.95**STEP
    update = moment1_new / first_fix / (jnp.sqrt(moment2_new / second_fix) + 1e-08)
    master_new = master * (1.0 - 0.02 * 0.1) - 0.02 * update
    return master_new, moment1_new, moment2_new


def new_states_kernel(mine, others, *refs):
    old, new = refs[:3], refs[3:]
    xh, y = lax.axis_index("xh"), lax.axis_index("y")
    for k in range(XH * Y // 2):
        for grad, low in ((mine[k], 0), (others[k], 1)):
            rows = pl.ds(pl.multiple_of((xh ^ (k % 2)) * LOW, LOW), LOW)
            at = (rows, pl.ds(pl.multiple_of((y ^ (k // 2 * 2 + low)) * COLS, 128), COLS))
            for ref, value in zip(new, adam(grad, *[ref[at] for ref in old])):
                ref[at] = value


def new_states(mine, others, master, moment1, moment2):
    return pl.pallas_call(
        new_states_kernel,
        out_shape=[jax.ShapeDtypeStruct(master.shape, master.dtype)] * 3,
        in_specs=[VMEM] * 5,
        out_specs=[VMEM] * 3,
        compiler_params=pltpu.CompilerParams(vmem_limit_bytes=8 * 2**20),
        cost_estimate=pl.CostEstimate(
            flops=20 * master.size, bytes_accessed=28 * master.size, transcendentals=master.size
        ),
        name="new_states",
    )(mine, others, master, moment1, moment2)


def exchange(chunks):
    return lax.all_to_all(chunks.reshape(-1, ZH, ZM, LOW, COLS), BIG, 0, 0, tiled=True)


def partner(a, axis, bit=1):
    return lax.ppermute(a, axis, [(i, i ^ bit) for i in range(lax.axis_size(axis))])


def halve(a, axis):
    return a[0] + partner(a[1].astype(jnp.float16), axis).astype(jnp.float32)


def add(parts):
    return jnp.sum(parts.astype(jnp.float32), axis=0)


def per_device(gradients, *states):
    rows, width = gradients.shape[2:]
    big = XH * Y * XL * ZL

    def in_hbm(a):
        return pltpu.with_memory_space_constraint(a, pltpu.HBM)

    whole = in_hbm(gradients.reshape(WHOLE))
    came = lax.ppermute(split_theirs(whole), "c", SWAP)
    pair, olds = split_mine(whole, *[in_hbm(state) for state in states])
    pair = pair.astype(jnp.float32) + came.astype(jnp.float32)
    column = add(exchange(pair.astype(jnp.float16)))

    grad = halve(halve(column, "zh"), "zm") / (big * ZH * ZM * CORES)

    part = adam(grad, *olds)[0].astype(jnp.bfloat16)
    mine = grad[None]
    part = jnp.stack([part, partner(part, "zm")])
    mine = jnp.concatenate([mine, partner(mine, "xh")])
    part, mine = lax.optimization_barrier((part, mine))
    part = jnp.stack([part, partner(part, "zh")])
    mine = jnp.concatenate([mine, partner(mine, "y", 2)])
    part, mine = lax.optimization_barrier((part, mine))
    part = exchange(jnp.broadcast_to(part, (big, *part.shape))).reshape(SHAPE)
    part, mine = lax.optimization_barrier((part, mine))
    came = lax.ppermute(part, "c", SWAP)
    others = partner(mine, "y", 1)
    params = place(True, came, (place(False, part),))
    return *new_states(mine, others, *states), params.reshape(rows, width)


def solution(mesh):
    sizes = (XH, Y, XL, ZH, ZM, ZL, CORES)
    fine = Mesh(mesh.devices.reshape(sizes), ("xh", "y", "xl", "zh", "zm", "zl", "c"))
    replica, shard = ("xh", "y"), ("xl", "zh", "zm", "zl", "c")
    state = P(shard, None)
    return jax.shard_map(
        per_device,
        mesh=fine,
        in_specs=(P(replica, shard, None, None), state, state, state),
        out_specs=(state, state, state, P()),
        check_vma=False,
    )
```

```python
import jax
import jax.numpy as jnp
from jax import lax
from jax.experimental import pallas as pl
from jax.experimental.pallas import tpu as pltpu
from jax.sharding import Mesh, PartitionSpec as P

STEP = 10
XH, Y, XL, ZH, ZM, ZL, CORES = 2, 4, 2, 2, 2, 2, 2
BIG = ("xh", "y", "xl", "zl")
SWAP = [(0, 1), (1, 0)]
LOW, COLS = 8, 1152
SHAPE = (XH, Y, XL, ZL, ZH, ZM, LOW, COLS)
WHOLE = (XL, ZH, ZM, ZL, CORES, XH, LOW, Y * COLS)
COPIES = XH * Y * ZH * ZM
STATES = 3
VMEM = pl.BlockSpec(memory_space=pltpu.VMEM)
ANY = pl.BlockSpec(memory_space=pl.ANY)
SMALL = pltpu.CompilerParams(vmem_limit_bytes=2 * 2**20)


def views(whole, pieces, core):
    zh, zm = lax.axis_index("zh"), lax.axis_index("zm")
    return [
        (whole.at[:, zh ^ j, zm ^ k, :, core, xh, :, pl.ds(y * COLS, COLS)], pieces.at[xh, y, :, :, j, k])
        for xh in range(XH)
        for y in range(Y)
        for j in range(ZH)
        for k in range(ZM)
    ]


def copy_all(pairs, sems):
    copies = [pltpu.make_async_copy(a, b, sems.at[k]) for k, (a, b) in enumerate(pairs)]
    for copy in copies:
        copy.start()
    for copy in copies:
        copy.wait()


def split_theirs_kernel(whole, pieces, sems):
    copy_all(views(whole, pieces, 1 - lax.axis_index("c")), sems)


def split_mine_kernel(whole, master, moment1, moment2, pieces, olds, sems):
    rows = pl.ds(pl.multiple_of(lax.axis_index("xh") * LOW, LOW), LOW)
    cols = pl.ds(pl.multiple_of(lax.axis_index("y") * COLS, 128), COLS)
    states = [(state.at[rows, cols], olds.at[i]) for i, state in enumerate((master, moment1, moment2))]
    copy_all(views(whole, pieces, lax.axis_index("c")) + states, sems)


def split_theirs(whole):
    return pl.pallas_call(
        split_theirs_kernel,
        out_shape=pltpu.VMEM(SHAPE, whole.dtype),
        in_specs=[ANY],
        out_specs=ANY,
        scratch_shapes=[pltpu.SemaphoreType.DMA((COPIES,))],
        compiler_params=SMALL,
        cost_estimate=pl.CostEstimate(flops=0, bytes_accessed=2 * whole.size, transcendentals=0),
        name="split_theirs",
    )(whole)


def split_mine(whole, *states):
    return pl.pallas_call(
        split_mine_kernel,
        out_shape=[pltpu.VMEM(SHAPE, whole.dtype), pltpu.VMEM((STATES, LOW, COLS), jnp.float32)],
        in_specs=[ANY] * (1 + STATES),
        out_specs=[ANY] * 2,
        scratch_shapes=[pltpu.SemaphoreType.DMA((COPIES + STATES,))],
        compiler_params=SMALL,
        cost_estimate=pl.CostEstimate(flops=0, bytes_accessed=2 * whole.size, transcendentals=0),
        name="split_mine",
    )(whole, *states)


def place_kernel(of_other, *refs):
    pieces, out, sems = refs[-3:]
    core = lax.axis_index("c")
    pairs = views(out, pieces, 1 - core if of_other else core)
    copy_all([(b, a) for a, b in pairs], sems)


def place(of_other, pieces, half=()):
    return pl.pallas_call(
        lambda *refs: place_kernel(of_other, *refs),
        out_shape=jax.ShapeDtypeStruct(WHOLE, pieces.dtype),
        in_specs=[ANY] * (len(half) + 1),
        out_specs=ANY,
        scratch_shapes=[pltpu.SemaphoreType.DMA((COPIES,))],
        input_output_aliases={0: 0} if half else {},
        compiler_params=SMALL,
        cost_estimate=pl.CostEstimate(flops=0, bytes_accessed=4 * pieces.size, transcendentals=0),
        name="place_theirs" if of_other else "place_mine",
    )(*half, pltpu.with_memory_space_constraint(pieces, pltpu.VMEM))


def adam(grad, master, moment1, moment2):
    moment1_new = 0.9 * moment1 + 0.1 * grad
    moment2_new = 0.95 * moment2 + 0.05 * grad * grad
    first_fix = 1.0 - 0.9**STEP
    second_fix = 1.0 - 0.95**STEP
    update = moment1_new / first_fix / (jnp.sqrt(moment2_new / second_fix) + 1e-08)
    master_new = master * (1.0 - 0.02 * 0.1) - 0.02 * update
    return master_new, moment1_new, moment2_new


def new_states_kernel(grads, *refs):
    old, new = refs[:STATES], refs[STATES:]
    for i in range(XH * Y):
        xh, y = divmod(i, Y)
        at = (pl.ds(xh * LOW, LOW), pl.ds(y * COLS, COLS))
        for ref, value in zip(new, adam(grads[i], *[ref[at] for ref in old])):
            ref[at] = value


def new_states(grads, *states):
    size = states[0].size
    return pl.pallas_call(
        new_states_kernel,
        out_shape=[jax.ShapeDtypeStruct(state.shape, state.dtype) for state in states],
        in_specs=[VMEM] * (1 + STATES),
        out_specs=[VMEM] * STATES,
        compiler_params=pltpu.CompilerParams(vmem_limit_bytes=8 * 2**20),
        cost_estimate=pl.CostEstimate(flops=20 * size, bytes_accessed=28 * size, transcendentals=size),
        name="new_states",
    )(grads, *states)


def exchange(chunks):
    return lax.all_to_all(chunks.reshape(-1, ZH * ZM, LOW, COLS), BIG, 0, 0, tiled=True)


def partner(a, m):
    return lax.ppermute(a, ("zh", "zm"), [(i, i ^ m) for i in range(ZH * ZM)])


def add(parts):
    return jnp.sum(parts.astype(jnp.float32), axis=0)


def per_device(gradients, *states):
    rows, width = gradients.shape[2:]
    big = XH * Y * XL * ZL

    def in_hbm(a):
        return pltpu.with_memory_space_constraint(a, pltpu.HBM)

    whole = in_hbm(gradients.reshape(WHOLE))
    came = lax.ppermute(split_theirs(whole), "c", SWAP)
    pair, olds = split_mine(whole, *[in_hbm(state) for state in states])
    pair = pair.astype(jnp.float32) + came.astype(jnp.float32)
    column = add(exchange(pair.astype(jnp.float16)))

    came = [partner(column[m].astype(jnp.float16), m) for m in range(1, ZH * ZM)]
    grad = sum((a.astype(jnp.float32) for a in came), column[0]) / (big * ZH * ZM * CORES)

    part = adam(grad, *olds)[0].astype(jnp.bfloat16)
    grads = lax.all_to_all(jnp.broadcast_to(grad, (XH * Y, LOW, COLS)), ("xh", "y"), 0, 0, tiled=True)
    part = jnp.stack([part] + [partner(part, m) for m in range(1, ZH * ZM)])
    part, grads = lax.optimization_barrier((part, grads))
    part = exchange(jnp.broadcast_to(part, (big, *part.shape))).reshape(SHAPE)
    part, grads = lax.optimization_barrier((part, grads))
    came = lax.ppermute(part, "c", SWAP)
    params = place(True, came, (place(False, part),))
    return *new_states(grads, *states), params.reshape(rows, width)


def solution(mesh):
    sizes = (XH, Y, XL, ZH, ZM, ZL, CORES)
    fine = Mesh(mesh.devices.reshape(sizes), ("xh", "y", "xl", "zh", "zm", "zl", "c"))
    replica, shard = ("xh", "y"), ("xl", "zh", "zm", "zl", "c")
    state = P(shard, None)
    return jax.shard_map(
        per_device,
        mesh=fine,
        in_specs=(P(replica, shard, None, None), state, state, state),
        out_specs=(state, state, state, P()),
        check_vma=False,
    )
```

```python
import jax
import jax.numpy as jnp
from jax import lax
from jax.experimental import pallas as pl
from jax.experimental.pallas import tpu as pltpu
from jax.sharding import Mesh, PartitionSpec as P

STEP = 10
XH, Y, XL, ZH, ZM, ZL, CORES = 2, 4, 2, 2, 2, 2, 2
BIG = ("xh", "y", "xl", "zl")
SWAP = [(0, 1), (1, 0)]
LOW, COLS = 8, 1152
SHAPE = (XH, Y, XL, ZL, ZH, ZM, LOW, COLS)
WHOLE = (XL, ZH, ZM, ZL, CORES, XH, LOW, Y * COLS)
COPIES = XH * Y * ZH * ZM
STATES = 3
VMEM = pl.BlockSpec(memory_space=pltpu.VMEM)
ANY = pl.BlockSpec(memory_space=pl.ANY)
SMALL = pltpu.CompilerParams(vmem_limit_bytes=2 * 2**20)


def views(whole, pieces, core):
    zh, zm = lax.axis_index("zh"), lax.axis_index("zm")
    return [
        (whole.at[:, zh ^ j, zm ^ k, :, core, xh, :, pl.ds(y * COLS, COLS)], pieces.at[xh, y, :, :, j, k])
        for xh in range(XH)
        for y in range(Y)
        for j in range(ZH)
        for k in range(ZM)
    ]


def copy_all(pairs, sems):
    copies = [pltpu.make_async_copy(a, b, sems.at[k]) for k, (a, b) in enumerate(pairs)]
    for copy in copies:
        copy.start()
    for copy in copies:
        copy.wait()


def split_theirs_kernel(whole, pieces, sems):
    copy_all(views(whole, pieces, 1 - lax.axis_index("c")), sems)


def split_mine_kernel(whole, master, moment1, moment2, pieces, olds, sems):
    rows = pl.ds(pl.multiple_of(lax.axis_index("xh") * LOW, LOW), LOW)
    cols = pl.ds(pl.multiple_of(lax.axis_index("y") * COLS, 128), COLS)
    states = [(state.at[rows, cols], olds.at[i]) for i, state in enumerate((master, moment1, moment2))]
    copy_all(views(whole, pieces, lax.axis_index("c")) + states, sems)


def split_theirs(whole):
    return pl.pallas_call(
        split_theirs_kernel,
        out_shape=pltpu.VMEM(SHAPE, whole.dtype),
        in_specs=[ANY],
        out_specs=ANY,
        scratch_shapes=[pltpu.SemaphoreType.DMA((COPIES,))],
        compiler_params=SMALL,
        cost_estimate=pl.CostEstimate(flops=0, bytes_accessed=2 * whole.size, transcendentals=0),
        name="split_theirs",
    )(whole)


def split_mine(whole, *states):
    return pl.pallas_call(
        split_mine_kernel,
        out_shape=[pltpu.VMEM(SHAPE, whole.dtype), pltpu.VMEM((STATES, LOW, COLS), jnp.float32)],
        in_specs=[ANY] * (1 + STATES),
        out_specs=[ANY] * 2,
        scratch_shapes=[pltpu.SemaphoreType.DMA((COPIES + STATES,))],
        compiler_params=SMALL,
        cost_estimate=pl.CostEstimate(flops=0, bytes_accessed=2 * whole.size, transcendentals=0),
        name="split_mine",
    )(whole, *states)


def place_kernel(of_other, *refs):
    pieces, out, sems = refs[-3:]
    core = lax.axis_index("c")
    pairs = views(out, pieces, 1 - core if of_other else core)
    copy_all([(b, a) for a, b in pairs], sems)


def place(of_other, pieces, half=()):
    return pl.pallas_call(
        lambda *refs: place_kernel(of_other, *refs),
        out_shape=jax.ShapeDtypeStruct(WHOLE, pieces.dtype),
        in_specs=[ANY] * (len(half) + 1),
        out_specs=ANY,
        scratch_shapes=[pltpu.SemaphoreType.DMA((COPIES,))],
        input_output_aliases={0: 0} if half else {},
        compiler_params=SMALL,
        cost_estimate=pl.CostEstimate(flops=0, bytes_accessed=4 * pieces.size, transcendentals=0),
        name="place_theirs" if of_other else "place_mine",
    )(*half, pltpu.with_memory_space_constraint(pieces, pltpu.VMEM))


def adam(grad, master, moment1, moment2):
    moment1_new = 0.9 * moment1 + 0.1 * grad
    moment2_new = 0.95 * moment2 + 0.05 * grad * grad
    first_fix = 1.0 - 0.9**STEP
    second_fix = 1.0 - 0.95**STEP
    update = moment1_new / first_fix / (jnp.sqrt(moment2_new / second_fix) + 1e-08)
    master_new = master * (1.0 - 0.02 * 0.1) - 0.02 * update
    return master_new, moment1_new, moment2_new


def new_states_kernel(early, late, *refs):
    old, new = refs[:STATES], refs[STATES:]
    xh, y, core = (lax.axis_index(a) for a in ("xh", "y", "c"))
    for k in range(XH * Y):
        grad = jnp.where(core == 0, early[k], late[k])
        rows = pl.ds(pl.multiple_of((xh ^ (k // Y)) * LOW, LOW), LOW)
        at = (rows, pl.ds(pl.multiple_of((y ^ (k % Y)) * COLS, 128), COLS))
        for ref, value in zip(new, adam(grad, *[ref[at] for ref in old])):
            ref[at] = value


def new_states(early, late, *states):
    size = states[0].size
    return pl.pallas_call(
        new_states_kernel,
        out_shape=[jax.ShapeDtypeStruct(state.shape, state.dtype) for state in states],
        in_specs=[VMEM] * (2 + STATES),
        out_specs=[VMEM] * STATES,
        compiler_params=pltpu.CompilerParams(vmem_limit_bytes=8 * 2**20),
        cost_estimate=pl.CostEstimate(flops=20 * size, bytes_accessed=28 * size, transcendentals=size),
        name="new_states",
    )(early, late, *states)


def exchange(chunks):
    return lax.all_to_all(chunks.reshape(-1, ZH * ZM, LOW, COLS), BIG, 0, 0, tiled=True)


def partner(a, m):
    return lax.ppermute(a, ("zh", "zm"), [(i, i ^ m) for i in range(ZH * ZM)])


def across(a, core, m):
    pairs = [(i * CORES + core, (i ^ m) * CORES + core) for i in range(XH * Y)]
    return lax.ppermute(a, ("xh", "y", "c"), pairs)


def pieces(grad, core):
    for m in (1, 2, 4):
        grad = jnp.concatenate([grad, across(grad, core, m)])
    return grad


def add(parts):
    return jnp.sum(parts.astype(jnp.float32), axis=0)


def per_device(gradients, *states):
    rows, width = gradients.shape[2:]
    big = XH * Y * XL * ZL

    def in_hbm(a):
        return pltpu.with_memory_space_constraint(a, pltpu.HBM)

    whole = in_hbm(gradients.reshape(WHOLE))
    came = lax.ppermute(split_theirs(whole), "c", SWAP)
    pair, olds = split_mine(whole, *[in_hbm(state) for state in states])
    pair = pair.astype(jnp.float32) + came.astype(jnp.float32)
    column = add(exchange(pair.astype(jnp.float16)))

    came = [partner(column[m].astype(jnp.float16), m) for m in range(1, ZH * ZM)]
    grad = sum((a.astype(jnp.float32) for a in came), column[0]) / (big * ZH * ZM * CORES)

    part = adam(grad, *olds)[0].astype(jnp.bfloat16)
    early = pieces(grad[None], 0)
    part = jnp.stack([part] + [partner(part, m) for m in range(1, ZH * ZM)])
    part, early, grad = lax.optimization_barrier((part, early, grad))
    part = exchange(jnp.broadcast_to(part, (big, *part.shape))).reshape(SHAPE)
    part, early, grad = lax.optimization_barrier((part, early, grad))
    late = pieces(grad[None], 1)
    part, early, late = lax.optimization_barrier((part, early, late))
    came = lax.ppermute(part, "c", SWAP)
    params = place(True, came, (place(False, part),))
    return *new_states(early, late, *states), params.reshape(rows, width)


def solution(mesh):
    sizes = (XH, Y, XL, ZH, ZM, ZL, CORES)
    fine = Mesh(mesh.devices.reshape(sizes), ("xh", "y", "xl", "zh", "zm", "zl", "c"))
    replica, shard = ("xh", "y"), ("xl", "zh", "zm", "zl", "c")
    state = P(shard, None)
    return jax.shard_map(
        per_device,
        mesh=fine,
        in_specs=(P(replica, shard, None, None), state, state, state),
        out_specs=(state, state, state, P()),
        check_vma=False,
    )
```

```python
import jax
import jax.numpy as jnp
from jax import lax
from jax.experimental import pallas as pl
from jax.experimental.pallas import tpu as pltpu
from jax.sharding import Mesh, PartitionSpec as P

STEP = 10
XH, Y, XL, ZH, ZM, ZL, CORES = 2, 4, 2, 2, 2, 2, 2
BIG = ("xh", "y", "xl", "zl")
SWAP = [(0, 1), (1, 0)]
LOW, COLS = 8, 1152
SHAPE = (XH, Y, XL, ZL, ZH, ZM, LOW, COLS)
WHOLE = (XL, ZH, ZM, ZL, CORES, XH, LOW, Y * COLS)
COPIES = XH * Y * ZH * ZM
STATES = 3
PAIR_SCALE, COLUMN_SCALE = 256.0, 8.0
VMEM = pl.BlockSpec(memory_space=pltpu.VMEM)
ANY = pl.BlockSpec(memory_space=pl.ANY)
SMALL = pltpu.CompilerParams(vmem_limit_bytes=2 * 2**20)


def views(whole, pieces, core):
    zh, zm = lax.axis_index("zh"), lax.axis_index("zm")
    return [
        (whole.at[:, zh ^ j, zm ^ k, :, core, xh, :, pl.ds(y * COLS, COLS)], pieces.at[xh, y, :, :, j, k])
        for xh in range(XH)
        for y in range(Y)
        for j in range(ZH)
        for k in range(ZM)
    ]


def copy_all(pairs, sems):
    copies = [pltpu.make_async_copy(a, b, sems.at[k]) for k, (a, b) in enumerate(pairs)]
    for copy in copies:
        copy.start()
    for copy in copies:
        copy.wait()


def split_theirs_kernel(whole, pieces, sems):
    copy_all(views(whole, pieces, 1 - lax.axis_index("c")), sems)


def split_mine_kernel(whole, master, moment1, moment2, pieces, olds, sems):
    rows = pl.ds(pl.multiple_of(lax.axis_index("xh") * LOW, LOW), LOW)
    cols = pl.ds(pl.multiple_of(lax.axis_index("y") * COLS, 128), COLS)
    states = [(state.at[rows, cols], olds.at[i]) for i, state in enumerate((master, moment1, moment2))]
    copy_all(views(whole, pieces, lax.axis_index("c")) + states, sems)


def split_theirs(whole):
    return pl.pallas_call(
        split_theirs_kernel,
        out_shape=pltpu.VMEM(SHAPE, whole.dtype),
        in_specs=[ANY],
        out_specs=ANY,
        scratch_shapes=[pltpu.SemaphoreType.DMA((COPIES,))],
        compiler_params=SMALL,
        cost_estimate=pl.CostEstimate(flops=0, bytes_accessed=2 * whole.size, transcendentals=0),
        name="split_theirs",
    )(whole)


def split_mine(whole, *states):
    return pl.pallas_call(
        split_mine_kernel,
        out_shape=[pltpu.VMEM(SHAPE, whole.dtype), pltpu.VMEM((STATES, LOW, COLS), jnp.float32)],
        in_specs=[ANY] * (1 + STATES),
        out_specs=[ANY] * 2,
        scratch_shapes=[pltpu.SemaphoreType.DMA((COPIES + STATES,))],
        compiler_params=SMALL,
        cost_estimate=pl.CostEstimate(flops=0, bytes_accessed=2 * whole.size, transcendentals=0),
        name="split_mine",
    )(whole, *states)


def place_kernel(of_other, *refs):
    pieces, out, sems = refs[-3:]
    core = lax.axis_index("c")
    pairs = views(out, pieces, 1 - core if of_other else core)
    copy_all([(b, a) for a, b in pairs], sems)


def place(of_other, pieces, half=()):
    return pl.pallas_call(
        lambda *refs: place_kernel(of_other, *refs),
        out_shape=jax.ShapeDtypeStruct(WHOLE, pieces.dtype),
        in_specs=[ANY] * (len(half) + 1),
        out_specs=ANY,
        scratch_shapes=[pltpu.SemaphoreType.DMA((COPIES,))],
        input_output_aliases={0: 0} if half else {},
        compiler_params=SMALL,
        cost_estimate=pl.CostEstimate(flops=0, bytes_accessed=4 * pieces.size, transcendentals=0),
        name="place_theirs" if of_other else "place_mine",
    )(*half, pltpu.with_memory_space_constraint(pieces, pltpu.VMEM))


def adam(grad, master, moment1, moment2):
    moment1_new = 0.9 * moment1 + 0.1 * grad
    moment2_new = 0.95 * moment2 + 0.05 * grad * grad
    first_fix = 1.0 - 0.9**STEP
    second_fix = 1.0 - 0.95**STEP
    update = moment1_new / first_fix / (jnp.sqrt(moment2_new / second_fix) + 1e-08)
    master_new = master * (1.0 - 0.02 * 0.1) - 0.02 * update
    return master_new, moment1_new, moment2_new


def new_states_kernel(grads, *refs):
    old, new = refs[:STATES], refs[STATES:]
    for i in range(XH * Y):
        xh, y = divmod(i, Y)
        at = (pl.ds(xh * LOW, LOW), pl.ds(y * COLS, COLS))
        for ref, value in zip(new, adam(grads[i], *[ref[at] for ref in old])):
            ref[at] = value


def new_states(grads, *states):
    size = states[0].size
    return pl.pallas_call(
        new_states_kernel,
        out_shape=[jax.ShapeDtypeStruct(state.shape, state.dtype) for state in states],
        in_specs=[VMEM] * (1 + STATES),
        out_specs=[VMEM] * STATES,
        compiler_params=pltpu.CompilerParams(vmem_limit_bytes=8 * 2**20),
        cost_estimate=pl.CostEstimate(flops=20 * size, bytes_accessed=28 * size, transcendentals=size),
        name="new_states",
    )(grads, *states)


def exchange(chunks):
    return lax.all_to_all(chunks.reshape(-1, ZH * ZM, LOW, COLS), BIG, 0, 0, tiled=True)


def partner(a, m):
    return lax.ppermute(a, ("zh", "zm"), [(i, i ^ m) for i in range(ZH * ZM)])


def add(parts):
    return jnp.sum(parts.astype(jnp.float32), axis=0)


def per_device(gradients, *states):
    rows, width = gradients.shape[2:]
    big = XH * Y * XL * ZL

    def in_hbm(a):
        return pltpu.with_memory_space_constraint(a, pltpu.HBM)

    whole = in_hbm(gradients.reshape(WHOLE))
    came = lax.ppermute(split_theirs(whole), "c", SWAP)
    pair, olds = split_mine(whole, *[in_hbm(state) for state in states])
    pair = pair.astype(jnp.float32) + came.astype(jnp.float32)
    column = add(exchange((PAIR_SCALE * pair).astype(jnp.float16))) * (COLUMN_SCALE / PAIR_SCALE)

    came = [partner(column[m].astype(jnp.float16), m) for m in range(1, ZH * ZM)]
    grad = sum((a.astype(jnp.float32) for a in came), column[0])
    grad = grad / (COLUMN_SCALE * big * ZH * ZM * CORES)

    part = adam(grad, *olds)[0].astype(jnp.bfloat16)
    grads = lax.all_to_all(jnp.broadcast_to(grad, (XH * Y, LOW, COLS)), ("xh", "y"), 0, 0, tiled=True)
    part = jnp.stack([part] + [partner(part, m) for m in range(1, ZH * ZM)])
    part, grads = lax.optimization_barrier((part, grads))
    part = exchange(jnp.broadcast_to(part, (big, *part.shape))).reshape(SHAPE)
    part, grads = lax.optimization_barrier((part, grads))
    came = lax.ppermute(part, "c", SWAP)
    params = place(True, came, (place(False, part),))
    return *new_states(grads, *states), params.reshape(rows, width)


def solution(mesh):
    sizes = (XH, Y, XL, ZH, ZM, ZL, CORES)
    fine = Mesh(mesh.devices.reshape(sizes), ("xh", "y", "xl", "zh", "zm", "zl", "c"))
    replica, shard = ("xh", "y"), ("xl", "zh", "zm", "zl", "c")
    state = P(shard, None)
    return jax.shard_map(
        per_device,
        mesh=fine,
        in_specs=(P(replica, shard, None, None), state, state, state),
        out_specs=(state, state, state, P()),
        check_vma=False,
    )
```

```python
import jax
import jax.numpy as jnp
from jax import lax
from jax.experimental import pallas as pl
from jax.experimental.pallas import tpu as pltpu
from jax.sharding import Mesh, PartitionSpec as P

STEP = 10
XH, Y, XL, ZH, ZM, ZL, CORES = 2, 4, 2, 2, 2, 2, 2
BIG = ("xh", "y", "xl", "zl")
SWAP = [(0, 1), (1, 0)]
LOW, COLS = 8, 1152
SHAPE = (XH, Y, XL, ZL, ZH, ZM, LOW, COLS)
WHOLE = (XL, ZH, ZM, ZL, CORES, XH, LOW, Y * COLS)
COPIES = XH * Y * ZH * ZM
STATES = 3
PAIR_SCALE, COLUMN_SCALE = 256.0, 8.0
BLOCKS = ZH * ZM
DEVICES = XH * Y * XL * ZL * ZH * ZM * CORES
VMEM = pl.BlockSpec(memory_space=pltpu.VMEM)
ANY = pl.BlockSpec(memory_space=pl.ANY)
SMALL = pltpu.CompilerParams(vmem_limit_bytes=2 * 2**20)


def views(whole, pieces, core):
    zh, zm = lax.axis_index("zh"), lax.axis_index("zm")
    return [
        (whole.at[:, zh ^ j, zm ^ k, :, core, xh, :, pl.ds(y * COLS, COLS)], pieces.at[xh, y, :, :, j, k])
        for xh in range(XH)
        for y in range(Y)
        for j in range(ZH)
        for k in range(ZM)
    ]


def copy_all(pairs, sems):
    copies = [pltpu.make_async_copy(a, b, sems.at[k]) for k, (a, b) in enumerate(pairs)]
    for copy in copies:
        copy.start()
    for copy in copies:
        copy.wait()


def split_theirs_kernel(whole, master, moment1, moment2, pieces, olds, sems):
    rows = pl.ds(pl.multiple_of(lax.axis_index("xh") * LOW, LOW), LOW)
    cols = pl.ds(pl.multiple_of(lax.axis_index("y") * COLS, 128), COLS)
    states = [(state.at[rows, cols], olds.at[i]) for i, state in enumerate((master, moment1, moment2))]
    copy_all(views(whole, pieces, 1 - lax.axis_index("c")) + states, sems)


def split_mine_kernel(whole, pieces, sems):
    copy_all(views(whole, pieces, lax.axis_index("c")), sems)


def split_theirs(whole, *states):
    return pl.pallas_call(
        split_theirs_kernel,
        out_shape=[pltpu.VMEM(SHAPE, whole.dtype), pltpu.VMEM((STATES, LOW, COLS), jnp.float32)],
        in_specs=[ANY] * (1 + STATES),
        out_specs=[ANY] * 2,
        scratch_shapes=[pltpu.SemaphoreType.DMA((COPIES + STATES,))],
        compiler_params=SMALL,
        cost_estimate=pl.CostEstimate(flops=0, bytes_accessed=2 * whole.size, transcendentals=0),
        name="split_theirs",
    )(whole, *states)


def split_mine(whole):
    return pl.pallas_call(
        split_mine_kernel,
        out_shape=pltpu.VMEM(SHAPE, whole.dtype),
        in_specs=[ANY],
        out_specs=ANY,
        scratch_shapes=[pltpu.SemaphoreType.DMA((COPIES,))],
        compiler_params=SMALL,
        cost_estimate=pl.CostEstimate(flops=0, bytes_accessed=2 * whole.size, transcendentals=0),
        name="split_mine",
    )(whole)


def place_kernel(of_other, *refs):
    pieces, out, sems = refs[-3:]
    core = lax.axis_index("c")
    pairs = views(out, pieces, 1 - core if of_other else core)
    copy_all([(b, a) for a, b in pairs], sems)


def place(of_other, pieces, half=()):
    return pl.pallas_call(
        lambda *refs: place_kernel(of_other, *refs),
        out_shape=jax.ShapeDtypeStruct(WHOLE, pieces.dtype),
        in_specs=[ANY] * (len(half) + 1),
        out_specs=ANY,
        scratch_shapes=[pltpu.SemaphoreType.DMA((COPIES,))],
        input_output_aliases={0: 0} if half else {},
        compiler_params=SMALL,
        cost_estimate=pl.CostEstimate(flops=0, bytes_accessed=4 * pieces.size, transcendentals=0),
        name="place_theirs" if of_other else "place_mine",
    )(*half, pltpu.with_memory_space_constraint(pieces, pltpu.VMEM))


def adam(grad, master, moment1, moment2):
    moment1_new = 0.9 * moment1 + 0.1 * grad
    moment2_new = 0.95 * moment2 + 0.05 * grad * grad
    first_fix = 1.0 - 0.9**STEP
    second_fix = 1.0 - 0.95**STEP
    update = moment1_new / first_fix / (jnp.sqrt(moment2_new / second_fix) + 1e-08)
    master_new = master * (1.0 - 0.02 * 0.1) - 0.02 * update
    return master_new, moment1_new, moment2_new


def new_states_kernel(grads, *refs):
    old, new = refs[:STATES], refs[STATES:]
    for i in range(XH * Y):
        xh, y = divmod(i, Y)
        at = (pl.ds(xh * LOW, LOW), pl.ds(y * COLS, COLS))
        for ref, value in zip(new, adam(grads[i], *[ref[at] for ref in old])):
            ref[at] = value


def new_states(grads, *states):
    size = states[0].size
    return pl.pallas_call(
        new_states_kernel,
        out_shape=[jax.ShapeDtypeStruct(state.shape, state.dtype) for state in states],
        in_specs=[VMEM] * (1 + STATES),
        out_specs=[VMEM] * STATES,
        compiler_params=pltpu.CompilerParams(vmem_limit_bytes=8 * 2**20),
        cost_estimate=pl.CostEstimate(flops=20 * size, bytes_accessed=28 * size, transcendentals=size),
        name="new_states",
    )(grads, *states)


def blocks_kernel(*refs):
    columns, olds, (params, grad) = refs[:BLOCKS], refs[BLOCKS : 2 * BLOCKS], refs[2 * BLOCKS :]
    for s in range(BLOCKS):
        near = columns[0][s] + columns[1][s ^ 1]
        far = columns[2][s ^ 2] + columns[3][s ^ 3]
        total = (near + far) / (COLUMN_SCALE * DEVICES)
        if s == 0:
            grad[...] = total
        old = olds[s]
        params[s] = adam(total, old[0], old[1], old[2])[0].astype(params.dtype)


def blocks(columns, olds):
    size = BLOCKS * LOW * COLS
    return pl.pallas_call(
        blocks_kernel,
        out_shape=[
            jax.ShapeDtypeStruct((BLOCKS, LOW, COLS), jnp.bfloat16),
            jax.ShapeDtypeStruct((LOW, COLS), jnp.float32),
        ],
        in_specs=[VMEM] * (2 * BLOCKS),
        out_specs=[VMEM] * 2,
        compiler_params=pltpu.CompilerParams(vmem_limit_bytes=8 * 2**20),
        cost_estimate=pl.CostEstimate(flops=20 * size, bytes_accessed=30 * size, transcendentals=size),
        name="blocks",
    )(*columns, *olds)


def spread_kernel(mine, *refs):
    theirs, out = refs[:-1], refs[-1]
    core = lax.axis_index("c")
    for s in range(BLOCKS):
        block = mine[s]
        if s:
            block = jnp.where(core == 0, block.astype(jnp.float32), theirs[s - 1][...].astype(jnp.float32))
            block = block.astype(out.dtype)
        for p in range(out.shape[0]):
            out[p, s] = block


def spread(mine, theirs):
    shape = (XH * Y * XL * ZL, BLOCKS, LOW, COLS)
    return pl.pallas_call(
        spread_kernel,
        out_shape=pltpu.VMEM(shape, mine.dtype),
        in_specs=[VMEM] * BLOCKS,
        out_specs=VMEM,
        compiler_params=pltpu.CompilerParams(vmem_limit_bytes=8 * 2**20),
        cost_estimate=pl.CostEstimate(flops=0, bytes_accessed=64 * mine.size, transcendentals=0),
        name="spread",
    )(mine, *theirs)


def exchange(chunks):
    return lax.all_to_all(chunks.reshape(-1, BLOCKS, LOW, COLS), BIG, 0, 0, tiled=True)


def partner(a, m, core=None):
    cores = range(CORES) if core is None else (core,)
    pairs = [(i * CORES + c, (i ^ m) * CORES + c) for i in range(BLOCKS) for c in cores]
    return lax.ppermute(a, ("zh", "zm", "c"), pairs)


def add(parts):
    return jnp.sum(parts.astype(jnp.float32), axis=0)


def per_device(gradients, *states):
    rows, width = gradients.shape[2:]
    partners = range(1, BLOCKS)

    def in_hbm(a):
        return pltpu.with_memory_space_constraint(a, pltpu.HBM)

    whole = in_hbm(gradients.reshape(WHOLE))
    theirs, old = split_theirs(whole, *[in_hbm(state) for state in states])
    came = lax.ppermute(theirs, "c", SWAP)
    far = partner(old, 2, 0)
    olds = [old, partner(old, 1, 0), far, partner(old, 3, 0)]
    pair = split_mine(whole).astype(jnp.float32) + came.astype(jnp.float32)
    pair, olds = lax.optimization_barrier(((PAIR_SCALE * pair).astype(jnp.float16), olds))

    column = add(exchange(pair)) * (COLUMN_SCALE / PAIR_SCALE)
    column = column.astype(jnp.float16)
    columns = [column] + [partner(column, m) for m in partners]
    mine, grad = blocks([a.astype(jnp.float32) for a in columns], olds)

    grads = lax.all_to_all(jnp.broadcast_to(grad, (XH * Y, LOW, COLS)), ("xh", "y"), 0, 0, tiled=True)
    theirs = [partner(mine[0], m, 1) for m in partners]
    mine, theirs, grads = lax.optimization_barrier((mine, theirs, grads))
    part = exchange(spread(mine, theirs)).reshape(SHAPE)
    part, grads = lax.optimization_barrier((part, grads))
    came = lax.ppermute(part, "c", SWAP)
    params = place(True, came, (place(False, part),))
    return *new_states(grads, *states), params.reshape(rows, width)


def solution(mesh):
    sizes = (XH, Y, XL, ZH, ZM, ZL, CORES)
    fine = Mesh(mesh.devices.reshape(sizes), ("xh", "y", "xl", "zh", "zm", "zl", "c"))
    replica, shard = ("xh", "y"), ("xl", "zh", "zm", "zl", "c")
    state = P(shard, None)
    return jax.shard_map(
        per_device,
        mesh=fine,
        in_specs=(P(replica, shard, None, None), state, state, state),
        out_specs=(state, state, state, P()),
        check_vma=False,
    )
```

```python
import jax
import jax.numpy as jnp
from jax import lax
from jax.experimental import pallas as pl
from jax.experimental.pallas import tpu as pltpu
from jax.sharding import Mesh, PartitionSpec as P

STEP = 10
XH, Y, XL, ZH, ZM, ZL, CORES = 2, 4, 2, 2, 2, 2, 2
BIG = ("xh", "y", "xl", "zl")
SWAP = [(0, 1), (1, 0)]
LOW, COLS = 8, 1152
SHAPE = (XH, Y, XL, ZL, ZH, ZM, LOW, COLS)
WHOLE = (XL, ZH, ZM, ZL, CORES, XH, LOW, Y * COLS)
STATES = 3
PAIR_SCALE, COLUMN_SCALE = 256.0, 8.0
VMEM = pl.BlockSpec(memory_space=pltpu.VMEM)
ANY = pl.BlockSpec(memory_space=pl.ANY)
SMALL = pltpu.CompilerParams(vmem_limit_bytes=2 * 2**20)


def views(whole, pieces, core):
    zh, zm = lax.axis_index("zh"), lax.axis_index("zm")
    return [
        (whole.at[:, zh ^ j, zm ^ k, :, core, xh, :, pl.ds(y * COLS, COLS)], pieces.at[xh, y, :, :, j, k])
        for xh in range(XH)
        for y in range(Y)
        for j in range(ZH)
        for k in range(ZM)
    ]


def copy_all(pairs, pieces, sem):
    for source, target in pairs:
        pltpu.make_async_copy(source, target, sem).start()
    pltpu.make_async_copy(pieces, pieces, sem).wait()


def split_theirs_kernel(whole, pieces, sem):
    copy_all(views(whole, pieces, 1 - lax.axis_index("c")), pieces, sem)


def split_mine_kernel(whole, master, moment1, moment2, pieces, olds, sem, sems):
    rows = pl.ds(pl.multiple_of(lax.axis_index("xh") * LOW, LOW), LOW)
    cols = pl.ds(pl.multiple_of(lax.axis_index("y") * COLS, 128), COLS)
    states = [(state.at[rows, cols], olds.at[i]) for i, state in enumerate((master, moment1, moment2))]
    copies = [pltpu.make_async_copy(a, b, sems.at[i]) for i, (a, b) in enumerate(states)]
    for copy in copies:
        copy.start()
    copy_all(views(whole, pieces, lax.axis_index("c")), pieces, sem)
    for copy in copies:
        copy.wait()


def split_theirs(whole):
    return pl.pallas_call(
        split_theirs_kernel,
        out_shape=pltpu.VMEM(SHAPE, whole.dtype),
        in_specs=[ANY],
        out_specs=ANY,
        scratch_shapes=[pltpu.SemaphoreType.DMA],
        compiler_params=SMALL,
        cost_estimate=pl.CostEstimate(flops=0, bytes_accessed=2 * whole.size, transcendentals=0),
        name="split_theirs",
    )(whole)


def split_mine(whole, *states):
    return pl.pallas_call(
        split_mine_kernel,
        out_shape=[pltpu.VMEM(SHAPE, whole.dtype), pltpu.VMEM((STATES, LOW, COLS), jnp.float32)],
        in_specs=[ANY] * (1 + STATES),
        out_specs=[ANY] * 2,
        scratch_shapes=[pltpu.SemaphoreType.DMA, pltpu.SemaphoreType.DMA((STATES,))],
        compiler_params=SMALL,
        cost_estimate=pl.CostEstimate(flops=0, bytes_accessed=2 * whole.size, transcendentals=0),
        name="split_mine",
    )(whole, *states)


def place_kernel(of_other, *refs):
    pieces, out, sem = refs[-3:]
    core = lax.axis_index("c")
    pairs = views(out, pieces, 1 - core if of_other else core)
    copy_all([(b, a) for a, b in pairs], pieces, sem)


def place(of_other, pieces, half=()):
    return pl.pallas_call(
        lambda *refs: place_kernel(of_other, *refs),
        out_shape=jax.ShapeDtypeStruct(WHOLE, pieces.dtype),
        in_specs=[ANY] * (len(half) + 1),
        out_specs=ANY,
        scratch_shapes=[pltpu.SemaphoreType.DMA],
        input_output_aliases={0: 0} if half else {},
        compiler_params=SMALL,
        cost_estimate=pl.CostEstimate(flops=0, bytes_accessed=4 * pieces.size, transcendentals=0),
        name="place_theirs" if of_other else "place_mine",
    )(*half, pltpu.with_memory_space_constraint(pieces, pltpu.VMEM))


def adam(grad, master, moment1, moment2):
    moment1_new = 0.9 * moment1 + 0.1 * grad
    moment2_new = 0.95 * moment2 + 0.05 * grad * grad
    first_fix = 1.0 - 0.9**STEP
    second_fix = 1.0 - 0.95**STEP
    update = moment1_new / first_fix / (jnp.sqrt(moment2_new / second_fix) + 1e-08)
    master_new = master * (1.0 - 0.02 * 0.1) - 0.02 * update
    return master_new, moment1_new, moment2_new


def new_states_kernel(grads, *refs):
    old, new = refs[:STATES], refs[STATES:]
    for i in range(XH * Y):
        xh, y = divmod(i, Y)
        at = (pl.ds(xh * LOW, LOW), pl.ds(y * COLS, COLS))
        for ref, value in zip(new, adam(grads[i], *[ref[at] for ref in old])):
            ref[at] = value


def new_states(grads, *states):
    size = states[0].size
    return pl.pallas_call(
        new_states_kernel,
        out_shape=[jax.ShapeDtypeStruct(state.shape, state.dtype) for state in states],
        in_specs=[VMEM] * (1 + STATES),
        out_specs=[VMEM] * STATES,
        compiler_params=pltpu.CompilerParams(vmem_limit_bytes=8 * 2**20),
        cost_estimate=pl.CostEstimate(flops=20 * size, bytes_accessed=28 * size, transcendentals=size),
        name="new_states",
    )(grads, *states)


def exchange(chunks):
    return lax.all_to_all(chunks.reshape(-1, ZH * ZM, LOW, COLS), BIG, 0, 0, tiled=True)


def partner(a, m):
    return lax.ppermute(a, ("zh", "zm"), [(i, i ^ m) for i in range(ZH * ZM)])


def add(parts):
    return jnp.sum(parts.astype(jnp.float32), axis=0)


def per_device(gradients, *states):
    rows, width = gradients.shape[2:]
    big = XH * Y * XL * ZL

    def in_hbm(a):
        return pltpu.with_memory_space_constraint(a, pltpu.HBM)

    whole = in_hbm(gradients.reshape(WHOLE))
    came = lax.ppermute(split_theirs(whole), "c", SWAP)
    pair, olds = split_mine(whole, *[in_hbm(state) for state in states])
    pair = pair.astype(jnp.float32) + came.astype(jnp.float32)
    column = add(exchange((PAIR_SCALE * pair).astype(jnp.float16))) * (COLUMN_SCALE / PAIR_SCALE)

    came = [partner(column[m].astype(jnp.float16), m) for m in range(1, ZH * ZM)]
    grad = sum((a.astype(jnp.float32) for a in came), column[0])
    grad = grad / (COLUMN_SCALE * big * ZH * ZM * CORES)

    part = adam(grad, *olds)[0].astype(jnp.bfloat16)
    grads = lax.all_to_all(jnp.broadcast_to(grad, (XH * Y, LOW, COLS)), ("xh", "y"), 0, 0, tiled=True)
    part = jnp.stack([part] + [partner(part, m) for m in range(1, ZH * ZM)])
    part, grads = lax.optimization_barrier((part, grads))
    part = exchange(jnp.broadcast_to(part, (big, *part.shape))).reshape(SHAPE)
    part, grads = lax.optimization_barrier((part, grads))
    came = lax.ppermute(part, "c", SWAP)
    params = place(True, came, (place(False, part),))
    return *new_states(grads, *states), params.reshape(rows, width)


def solution(mesh):
    sizes = (XH, Y, XL, ZH, ZM, ZL, CORES)
    fine = Mesh(mesh.devices.reshape(sizes), ("xh", "y", "xl", "zh", "zm", "zl", "c"))
    replica, shard = ("xh", "y"), ("xl", "zh", "zm", "zl", "c")
    state = P(shard, None)
    return jax.shard_map(
        per_device,
        mesh=fine,
        in_specs=(P(replica, shard, None, None), state, state, state),
        out_specs=(state, state, state, P()),
        check_vma=False,
    )
```
